32 devices in a mesh: groups: 2 (over x), genome: 16 (over z, y, core).
Axes of the slice: x: 2, y: 2, z: 4, core: 2. Of those that a mesh axis runs over, the one named last changes fastest.
Arguments:
- factor: bfloat16 [96, 2048, 256], P(('groups', 'genome')), parts along dimension 0, may hold values from -0.5 to 0.5
- normals: bfloat16 [96, 256, 1024], P(('groups', 'genome')), parts along dimension 0, may hold values from -6 to 6
- block_len: int32 [96], P(('groups', 'genome')), parts along dimension 0, may hold values from 256 to 2048, as said below
- block_rank: int32 [96], P(('groups', 'genome')), parts along dimension 0, may hold values from 32 to 256, as said below
- gene_span: int32 [2048, 2], P(('groups', 'genome')), parts along dimension 0, may hold values from 0 to 98304, as said below
- gene_pathways: int32 [2048, 4], P('groups'), parts along dimension 0, may hold values from 0 to 4095, as said below
Outputs:
- pathway_score: float32 [8192, 1024], P(('groups', 'genome')), parts along dimension 0
The draws below stay inside these ranges and needn't reach their ends.
There are 2 independent parts, one for each index of `groups`. The reference program is written for one: setup_inputs(seed, part) draws one part's arguments, and reference() takes and returns one part's arrays. A program takes and returns all parts, laid end to end along the dimension named above; each array names one. Nothing has to cross between parts.
Inputs may be any that keep to these rules, and one draw needn't show every extreme that they name: `block_len`: some block of every draw holds all 2048 slots. `block_rank`: some block of every draw keeps all 256 columns. `gene_span`: genes of rows j * 64 to (j + 1) * 64 - 1 start at a valid slot within slots j * 6144 to (j + 1) * 6144 - 1 and end no later than (j + 1) * 6144 + 2048, never past 98304; the end exceeds the start; some gene of every draw ends exactly 2048 slots past the range of its start. Each gene names 4 different pathways, and every pathway is named by some gene. With q = g * 4 + m, the pathway gene_pathways[g, m] lies in rows r * 256 to (r + 1) * 256 - 1 with r = q % 16, so the genes of one index of genome name at most 16 pathways of one such range, and exactly 16 for some range.
All inputs are finite; a program needn't handle non-finite values.
Results may differ from the reference program's by a relative error of at most 0.0021.
Values may be sent and summed in bfloat16 or wider, within the bound.
A program may use at most 128 MiB of HBM per device.

```python
import jax
import jax.numpy as jnp
from jax import lax

BLK_DEV = 3
BVAR = 2048
RANK = 256
SIMS = 1024
GENES_DEV = 64
PATHWAYS = 4096
MEMB = 4
BLOCKS = 48
VAR_DEV = 6144
VARIANTS = 98304
GENES = 1024
N_GENOME = 16


def make_layout(key):
    layout_key = jax.random.fold_in(key, 7)
    keys = jax.random.split(layout_key, 6)
    lengths = jax.random.randint(keys[0], (BLOCKS,), BVAR // 8, BVAR + 1)
    fullest = jax.random.randint(keys[1], (), 0, BLOCKS)
    lengths = jnp.where(jnp.arange(BLOCKS) == fullest, BVAR, lengths).astype(jnp.int32)
    device_count = BLOCKS // BLK_DEV
    shape = (device_count, GENES_DEV)
    device_ids = jnp.arange(device_count, dtype=jnp.int32)[:, None] + jnp.zeros(shape, jnp.int32)
    gene_ids = jnp.arange(GENES_DEV, dtype=jnp.int32)[None, :] + jnp.zeros(shape, jnp.int32)
    straddle = (gene_ids == GENES_DEV - 1) & (device_ids < device_count - 1)
    slots = jax.random.randint(keys[2], shape, 0, BLK_DEV)
    slots = jnp.where(straddle, BLK_DEV - 1, slots)
    block_ids = device_ids * BLK_DEV + slots
    block_sizes = jnp.take(lengths, block_ids)
    rows_in = jax.random.randint(keys[3], shape, 0, block_sizes)
    starts = block_ids * BVAR + rows_in
    widths = jax.random.randint(keys[4], shape, BVAR // 4, 2 * BVAR)
    device_end = (device_ids + 1) * VAR_DEV
    inner_end = jnp.minimum(starts + widths, device_end)
    reach = jax.random.randint(keys[5], shape, 1, BVAR + 1)
    reach = jnp.where(device_ids == 0, BVAR, reach)
    ends = jnp.where(straddle, device_end + reach, inner_end)
    spans = jnp.stack([starts, ends], axis=-1).reshape(device_count * GENES_DEV, 2).astype(jnp.int32)
    return (lengths, spans)


def draw_block_len(key, part):
    return make_layout(key)[0]


def draw_gene_span(key, part):
    return make_layout(key)[1]


def draw_block_rank(key, part):
    rank_key = jax.random.fold_in(key, 9)
    first_key, second_key = jax.random.split(rank_key)
    ranks = jax.random.randint(first_key, (BLOCKS,), RANK // 8, RANK + 1)
    fullest = jax.random.randint(second_key, (), 0, BLOCKS)
    return jnp.where(jnp.arange(BLOCKS) == fullest, RANK, ranks).astype(jnp.int32)


def draw_gene_pathways(key, part):
    member_key = jax.random.fold_in(key, 11)
    first_key, second_key = jax.random.split(member_key)
    device_count = GENES // GENES_DEV
    path_rows = PATHWAYS // device_count
    pairs = jnp.arange(GENES * MEMB, dtype=jnp.int32)
    owner = pairs % device_count
    order = pairs // device_count
    perms = jax.vmap(lambda single: jax.random.permutation(single, path_rows))(jax.random.split(first_key, device_count))
    extra = jax.random.randint(second_key, (GENES * MEMB,), 0, path_rows)
    picked = perms[owner, order % path_rows]
    local = jnp.where(order < path_rows, picked, extra)
    return (owner * path_rows + local).reshape(GENES, MEMB).astype(jnp.int32)


def level_of(own_key, dims, pieces, low, top_value):
    level = 1.0
    for axis_at, blocks in pieces:
        heights = jax.random.uniform(jax.random.fold_in(jax.random.fold_in(own_key, 6), axis_at), (blocks,), jnp.float32, low / len(pieces), top_value / len(pieces))
        level = level * jnp.repeat(jnp.exp(heights), dims[axis_at] // blocks).reshape((-1,) + (1,) * (len(dims) - 1 - axis_at))
    return level


def scatter_about(rng, shape, spread, bound, shards=(), kind=jnp.bfloat16):
    loudness = level_of(rng, shape, shards, -0.22, 0.18) if shards else 1.0
    drawn = jax.random.normal(rng, shape, jnp.float32) * spread * loudness
    return jnp.minimum(jnp.maximum(drawn, -bound), bound).astype(kind)


def setup_inputs(seed: int = 0, part: int = 0) -> dict:
    key_list = jax.random.split(jax.random.key(seed), 7)
    own_keys = jax.random.split(jax.random.fold_in(key_list[6], part), 7)
    factor = scatter_about(own_keys[0], (BLOCKS, BVAR, RANK), (RANK // 2) ** -0.5, 0.5, ((0, 16),))
    normals = scatter_about(own_keys[1], (BLOCKS, RANK, SIMS), 1.0, 6.0, ((0, 16),))
    block_len = draw_block_len(jax.random.fold_in(jax.random.fold_in(key_list[6], part), 71), part)
    block_rank = draw_block_rank(jax.random.fold_in(jax.random.fold_in(key_list[6], part), 71), part)
    gene_span = draw_gene_span(jax.random.fold_in(jax.random.fold_in(key_list[6], part), 71), part)
    gene_pathways = draw_gene_pathways(jax.random.fold_in(jax.random.fold_in(key_list[6], part), 71), part)
    return dict(factor=factor, normals=normals, block_len=block_len, block_rank=block_rank, gene_span=gene_span, gene_pathways=gene_pathways)


def covered(positions, spans):
    lower = spans[:, 0][:, None]
    upper = spans[:, 1][:, None]
    return ((positions[None, :] >= lower) & (positions[None, :] < upper)).astype(jnp.float32)


def reference(factor, normals, block_len, block_rank, gene_span, gene_pathways):
    def device_sums(index):
        chosen = jnp.minimum(index * BLK_DEV + jnp.arange(BLK_DEV + 1, dtype=jnp.int32), BLOCKS - 1).astype(jnp.int32)
        factors = jnp.take(factor, chosen, axis=0).astype(jnp.float32)
        vectors = jnp.take(normals, chosen, axis=0).astype(jnp.float32)
        ranks = jnp.take(block_rank, chosen, axis=0)
        lengths = jnp.take(block_len, chosen, axis=0)
        kept = jnp.arange(RANK, dtype=jnp.int32)[None, :, None] < ranks[:, None, None]
        vectors = jnp.where(kept, vectors, jnp.zeros_like(vectors))
        coloured = jnp.einsum("bvk,bks->bvs", factors, vectors, precision=lax.Precision.HIGHEST)
        positions = index * VAR_DEV + jnp.arange((BLK_DEV + 1) * BVAR, dtype=jnp.int32)
        usable = (jnp.arange(BVAR, dtype=jnp.int32)[None, :] < lengths[:, None]).reshape(-1)
        usable = usable & (positions < VARIANTS)
        squares = jnp.where(usable[:, None], (coloured * coloured).reshape((BLK_DEV + 1) * BVAR, SIMS), 0.0)
        spans = lax.dynamic_slice_in_dim(gene_span, (index * GENES_DEV).astype(jnp.int32), GENES_DEV, 0)
        return jnp.dot(covered(positions, spans), squares, precision=lax.Precision.HIGHEST)

    totals = lax.map(device_sums, jnp.arange(N_GENOME, dtype=jnp.int32)).reshape(GENES, SIMS)
    gene_stat = (totals / BVAR).astype(jnp.bfloat16)
    member = jnp.any(gene_pathways[:, :, None] == jnp.arange(PATHWAYS, dtype=jnp.int32)[None, None, :], axis=1)
    path_count = jnp.sum(member.astype(jnp.float32), axis=0)
    path_sum = jnp.dot(member.astype(jnp.bfloat16).T, gene_stat, preferred_element_type=jnp.float32)
    return path_sum / path_count[:, None]
```

```python
import functools

import jax
import jax.numpy as jnp
from jax import lax
from jax.experimental import pallas as pl
from jax.experimental.pallas import tpu as pltpu
from jax.sharding import PartitionSpec as P

PATHWAYS = 4096
TILE = 512
QUAD = 4


def kernel(
    n, genes, rows,
    len_ref, rank_ref, span_ref, paths_ref, factor_ref, normals_ref,
    out_ref,
    fac, nrm, sums, partial, halo, own_span, pred_span, stat, gathered, member, count,
    fac_sem, nrm_sem, span_send, span_recv, halo_send, halo_recv,
    col_send, col_recv, quad_send, quad_recv,
):
    quads = n // QUAD
    blocks, capacity, rank_cap = factor_ref.shape
    sims = normals_ref.shape[2]
    local_vars = blocks * capacity
    padded = quads * rows
    me = lax.axis_index("genome")
    right, left = lax.rem(me + 1, n), lax.rem(me + n - 1, n)
    quad, lane = me // QUAD, lax.rem(me, QUAD)
    column = [lax.rem(quad + d, quads) * QUAD + lane for d in range(1, quads)]
    peers = [quad * QUAD + lax.rem(lane + e, QUAD) for e in range(1, QUAD)]

    order = [1, 0, 2] if blocks == 3 else list(range(1, blocks)) + [0]
    fac_copies, nrm_copies = {}, {}
    for b in order:
        nrm_copies[b] = pltpu.make_async_copy(normals_ref.at[b], nrm.at[b], nrm_sem.at[b])
        fac_copies[b] = pltpu.make_async_copy(factor_ref.at[b], fac.at[b], fac_sem.at[b])
        nrm_copies[b].start()
        fac_copies[b].start()

    barrier = pltpu.get_barrier_semaphore()
    greeted = [left, right] + column + peers
    for device in greeted:
        pl.semaphore_signal(barrier, inc=1, device_id={"genome": device})

    share = genes // quads
    row = lax.broadcasted_iota(jnp.int32, (padded, genes), 0)
    col = lax.broadcasted_iota(jnp.int32, (padded, genes), 1)
    within = row % rows
    placed = (row // rows + quads * within == col) & (within < share)

    def columns_of(spans):
        lower = jnp.sum(jnp.where(placed, spans[0:1, :genes], 0.0), axis=1, keepdims=True)
        upper = jnp.sum(jnp.where(placed, spans[1:2, :genes], 0.0), axis=1, keepdims=True)
        return lower.astype(jnp.int32), upper.astype(jnp.int32)

    own_span[...] = jnp.zeros_like(own_span)
    own_span[0:2, 0:genes] = span_ref[...].astype(jnp.float32)
    lower, upper = columns_of(own_span[...])
    sums[...] = jnp.zeros_like(sums)

    def trim(b):
        nrm_copies[b].wait()
        ids = lax.broadcasted_iota(jnp.int32, (rank_cap, sims), 0)
        values = nrm[b].astype(jnp.float32)
        nrm[b] = jnp.where(ids < rank_ref[b], values, 0.0).astype(jnp.bfloat16)

    def add_tile(b, step, spans):
        first = step * TILE
        coloured = jnp.dot(
            fac[b, pl.ds(first, TILE), :], nrm[b], preferred_element_type=jnp.float32
        )
        squares = (coloured * coloured).astype(jnp.bfloat16)
        start = me * local_vars + b * capacity
        limit = start + len_ref[b]
        for into, low, high in spans:
            place = start + first + lax.broadcasted_iota(jnp.int32, (padded, TILE), 1)
            inside = (place >= low) & (place < jnp.minimum(high, limit))
            into[...] += jnp.dot(
                inside.astype(jnp.float32).astype(jnp.bfloat16),
                squares,
                preferred_element_type=jnp.float32,
            )

    def add_block(b, spans, begin=0, end=None):
        for step in range(begin, capacity // TILE if end is None else end):
            add_tile(b, step, spans)

    own = [(sums, lower, upper)]
    b = order[0]
    trim(b)
    fac_copies[b].wait()
    half = capacity // TILE // 2
    add_block(b, own, 0, half)
    pl.semaphore_wait(barrier, len(greeted))
    span_copy = pltpu.make_async_remote_copy(
        own_span, pred_span, span_send, span_recv, device_id={"genome": right}
    )
    span_copy.start()
    add_block(b, own, half)
    for b in order[1:]:
        trim(b)
        fac_copies[b].wait()
        if b == 0:
            span_copy.wait()
            partial[...] = jnp.zeros_like(partial)
            pred_lower, pred_upper = columns_of(pred_span[...])
            add_block(b, own + [(partial, pred_lower, pred_upper)])
            halo_copy = pltpu.make_async_remote_copy(
                partial, halo, halo_send, halo_recv, device_id={"genome": left}
            )

            @pl.when(me > 0)
            def _():
                halo_copy.start()
        else:
            add_block(b, own)

    path_rows, total_genes = out_ref.shape[0], paths_ref.shape[1]
    slots = n * rows
    named = paths_ref[pl.ds(lane, 1), :] - me * path_rows
    ids = lax.broadcasted_iota(jnp.int32, (path_rows, total_genes), 0)
    names = (named == ids).astype(jnp.float32).astype(jnp.bfloat16)
    gene = lax.broadcasted_iota(jnp.int32, (total_genes, slots), 0)
    slot = lax.broadcasted_iota(jnp.int32, (total_genes, slots), 1)
    takes = (gene // genes) * rows + (gene % genes) // quads == slot
    chosen = jnp.dot(
        names, takes.astype(jnp.float32).astype(jnp.bfloat16), preferred_element_type=jnp.float32
    )
    count[...] = jnp.sum(chosen, axis=1, keepdims=True)
    member[...] = chosen.astype(jnp.bfloat16)

    scale = 1.0 / capacity

    @pl.when(me < n - 1)
    def _():
        halo_copy.wait_recv()
        stat[...] = ((sums[...] + halo[...]) * scale).astype(jnp.bfloat16)

    @pl.when(me == n - 1)
    def _():
        stat[...] = (sums[...] * scale).astype(jnp.bfloat16)

    @pl.when(me > 0)
    def _():
        halo_copy.wait_send()

    sent = []
    for d in range(1, quads):
        target = lax.rem(quad + d, quads)
        copy = pltpu.make_async_remote_copy(
            stat.at[pl.ds(pl.multiple_of(target * rows, rows), rows)],
            gathered.at[pl.ds(pl.multiple_of(me * rows, rows), rows)],
            col_send.at[d], col_recv.at[d],
            device_id={"genome": target * QUAD + lane},
        )
        copy.start()
        sent.append(copy)
    gathered[pl.ds(pl.multiple_of(me * rows, rows), rows), :] = stat[
        pl.ds(pl.multiple_of(quad * rows, rows), rows), :
    ]

    def forward(d):
        source = lax.rem(quad + quads - d, quads) * QUAD + lane
        block = gathered.at[pl.ds(pl.multiple_of(source * rows, rows), rows)]
        for e in range(1, QUAD):
            copy = pltpu.make_async_remote_copy(
                block, block, quad_send.at[d, e], quad_recv.at[d, e],
                device_id={"genome": peers[e - 1]},
            )
            copy.start()
            sent.append(copy)

    forward(0)
    for d in range(1, quads):
        sent[d - 1].wait_recv()
        forward(d)
    for copy in sent[quads - 1:]:
        copy.wait_recv()
    summed = jnp.dot(member[...], gathered[...], preferred_element_type=jnp.float32)
    out_ref[...] = summed / count[...]
    for copy in sent:
        copy.wait_send()


def local(factor, normals, block_len, block_rank, gene_span, gene_pathways):
    blocks, capacity, rank_cap = factor.shape
    sims = normals.shape[2]
    genes = gene_span.shape[0]
    n = lax.axis_size("genome")
    quads = n // QUAD
    rows = max(16, genes // quads)
    padded = quads * rows
    path_rows = PATHWAYS // n
    vmem = pl.BlockSpec(memory_space=pltpu.VMEM)
    smem = pl.BlockSpec(memory_space=pltpu.SMEM)
    hbm = pl.BlockSpec(memory_space=pl.ANY)
    dma = pltpu.SemaphoreType.DMA
    return pl.pallas_call(
        functools.partial(kernel, n, genes, rows),
        out_shape=jax.ShapeDtypeStruct((path_rows, sims), jnp.float32),
        in_specs=[smem, smem, vmem, vmem, hbm, hbm],
        out_specs=vmem,
        scratch_shapes=[
            pltpu.VMEM((blocks, capacity, rank_cap), jnp.bfloat16),
            pltpu.VMEM((blocks, rank_cap, sims), jnp.bfloat16),
            pltpu.VMEM((padded, sims), jnp.float32),
            pltpu.VMEM((padded, sims), jnp.float32),
            pltpu.VMEM((padded, sims), jnp.float32),
            pltpu.VMEM((8, 128), jnp.float32),
            pltpu.VMEM((8, 128), jnp.float32),
            pltpu.VMEM((padded, sims), jnp.bfloat16),
            pltpu.VMEM((n * rows, sims), jnp.bfloat16),
            pltpu.VMEM((path_rows, n * rows), jnp.bfloat16),
            pltpu.VMEM((path_rows, 1), jnp.float32),
            dma((blocks,)), dma((blocks,)), dma, dma, dma, dma,
            dma((quads,)), dma((quads,)), dma((quads, QUAD)), dma((quads, QUAD)),
        ],
        compiler_params=pltpu.CompilerParams(
            collective_id=0, has_side_effects=True, vmem_limit_bytes=50 * 1024 * 1024
        ),
        name="gene_sets",
    )(block_len, block_rank, gene_span.T, gene_pathways.T, factor, normals)


def solution(mesh):
    in_specs = (
        P(("groups", "genome"), None, None),
        P(("groups", "genome"), None, None),
        P(("groups", "genome")),
        P(("groups", "genome")),
        P(("groups", "genome"), None),
        P("groups", None),
    )
    out_specs = P(("groups", "genome"), None)
    return jax.shard_map(local, mesh=mesh, in_specs=in_specs, out_specs=out_specs, check_vma=False)
```

```python
import functools

import jax
import jax.numpy as jnp
from jax import lax
from jax.experimental import pallas as pl
from jax.experimental.pallas import tpu as pltpu
from jax.sharding import PartitionSpec as P

PATHWAYS = 4096
PIECE = 256
TILE = 1024
QUAD = 4


def kernel(
    n, genes, rows,
    len_hbm, rank_hbm, span_hbm, paths_hbm, factor_ref, normals_ref,
    out_ref,
    len_ref, rank_ref, span_ref, paths_ref, fac, nrm, cover, cover_both,
    sums, partial, halo, own_span, pred_span, stat, gathered, member, count, result,
    small_sem, fac_sem, nrm_sem, span_send, span_recv, halo_send, halo_recv,
    col_send, col_recv, quad_send, quad_recv, out_sem,
):
    quads = n // QUAD
    blocks, capacity, rank_cap = factor_ref.shape
    sims = normals_ref.shape[2]
    pieces = sims // PIECE
    local_vars = blocks * capacity
    padded = quads * rows
    path_rows, total_genes = out_ref.shape[0], paths_ref.shape[1]
    slots = n * rows
    me = lax.axis_index("genome")
    right, left = lax.rem(me + 1, n), lax.rem(me + n - 1, n)
    quad, lane = me // QUAD, lax.rem(me, QUAD)
    column = [lax.rem(quad + d, quads) * QUAD + lane for d in range(1, quads)]
    peers = [quad * QUAD + lax.rem(lane + e, QUAD) for e in range(1, QUAD)]

    barrier = pltpu.get_barrier_semaphore()
    greeted = [left, right] + column + peers
    for device in greeted:
        pl.semaphore_signal(barrier, inc=1, device_id={"genome": device})

    small = [
        pltpu.make_async_copy(source, target, small_sem.at[i])
        for i, (source, target) in enumerate(
            [(span_hbm, span_ref), (rank_hbm, rank_ref), (len_hbm, len_ref), (paths_hbm, paths_ref)]
        )
    ]
    for copy in small:
        copy.start()
    order = list(range(1, blocks)) + [0]
    fac_copies, nrm_copies = {}, {}
    for b in order:
        nrm_copies[b] = pltpu.make_async_copy(normals_ref.at[b], nrm.at[b], nrm_sem.at[b])
        fac_copies[b] = pltpu.make_async_copy(factor_ref.at[b], fac.at[b], fac_sem.at[b])
        nrm_copies[b].start()
        fac_copies[b].start()

    share = genes // quads
    row = lax.broadcasted_iota(jnp.int32, (padded, genes), 0)
    col = lax.broadcasted_iota(jnp.int32, (padded, genes), 1)
    within = lax.rem(row, rows)
    placed = (lax.div(row, rows) + quads * within == col) & (within < share)

    def columns_of(spans):
        lower = jnp.sum(jnp.where(placed, spans[0:1, :genes], 0.0), axis=1, keepdims=True)
        upper = jnp.sum(jnp.where(placed, spans[1:2, :genes], 0.0), axis=1, keepdims=True)
        return lower.astype(jnp.int32), upper.astype(jnp.int32)

    slot = lax.broadcasted_iota(jnp.int32, (1, slots), 1)
    first_gene = lax.div(slot, rows) * genes + lax.rem(slot, rows) * quads
    first_gene = jnp.where(lax.rem(slot, rows) < share, first_gene, total_genes)
    gene = lax.broadcasted_iota(jnp.int32, (total_genes, slots), 0)
    takes = (gene >= first_gene) & (gene < first_gene + quads)
    takes = takes.astype(jnp.float32).astype(jnp.bfloat16)
    own_span[...] = jnp.zeros_like(own_span)
    for copy in small:
        copy.wait()
    own_span[0:2, 0:genes] = span_ref[...].astype(jnp.float32)
    lower, upper = columns_of(own_span[...])
    named = paths_ref[pl.ds(lane, 1), :] - me * path_rows
    ids = lax.broadcasted_iota(jnp.int32, (path_rows, total_genes), 0)
    names = (named == ids).astype(jnp.float32).astype(jnp.bfloat16)
    chosen = jnp.dot(names, takes, preferred_element_type=jnp.float32)
    count[...] = jnp.sum(chosen, axis=1, keepdims=True)
    member[...] = chosen.astype(jnp.bfloat16)

    def trim(b):
        nrm_copies[b].wait()
        kept = lax.broadcasted_iota(jnp.int32, (rank_cap, sims), 0) < rank_ref[b]
        nrm[b] = jnp.where(kept, nrm[b].astype(jnp.float32), 0.0).astype(jnp.bfloat16)

    def coverage(b, low, high):
        start = me * local_vars + b * capacity
        place = start + lax.broadcasted_iota(jnp.int32, (padded, capacity), 1)
        inside = (place >= low) & (place < jnp.minimum(high, start + len_ref[b]))
        return inside.astype(jnp.float32).astype(jnp.bfloat16)

    def coloured(b, piece, first):
        return jnp.dot(
            fac[b, pl.ds(first, TILE), :],
            nrm[b, :, pl.ds(piece * PIECE, PIECE)],
            preferred_element_type=jnp.float32,
        )

    def add_blocks(chain, piece):
        steps = [(b, first) for b in chain for first in range(0, capacity, TILE)]
        totals = {}
        ahead = coloured(steps[0][0], piece, steps[0][1])
        for at, (b, first) in enumerate(steps):
            squares = (ahead * ahead).astype(jnp.bfloat16)
            if at + 1 < len(steps):
                ahead = coloured(steps[at + 1][0], piece, steps[at + 1][1])
            rows_of = cover_both if b == 0 else cover.at[b]
            term = jnp.dot(
                rows_of[:, pl.ds(first, TILE)], squares, preferred_element_type=jnp.float32
            )
            totals[b] = totals[b] + term if b in totals else term
        kept = None
        for b, total in totals.items():
            if b == 0:
                partial[piece] = total[padded:]
                total = total[:padded]
            kept = total if kept is None else kept + total
        return kept

    halo_copies = [
        pltpu.make_async_remote_copy(
            partial.at[piece], halo.at[piece], halo_send.at[piece], halo_recv.at[piece],
            device_id={"genome": left},
        )
        for piece in range(pieces)
    ]

    def send_halo(piece):
        @pl.when(me > 0)
        def _():
            halo_copies[piece].start()

    scale = 1.0 / capacity
    col_copies, quad_copies = {}, {}

    def slot_rows(index):
        return pl.ds(pl.multiple_of(index * rows, rows), rows)

    def forward(piece, d):
        source = lax.rem(quad + quads - d, quads) * QUAD + lane
        block = gathered.at[piece, slot_rows(source)]
        for e in range(1, QUAD):
            copy = pltpu.make_async_remote_copy(
                block, block, quad_send.at[piece, d, e], quad_recv.at[piece, d, e],
                device_id={"genome": peers[e - 1]},
            )
            copy.start()
            quad_copies[piece, d, e] = copy

    def finish_stat(piece):
        @pl.when(me < n - 1)
        def _():
            halo_copies[piece].wait_recv()
            stat[piece] = ((sums[piece] + halo[piece]) * scale).astype(jnp.bfloat16)

        @pl.when(me == n - 1)
        def _():
            stat[piece] = (sums[piece] * scale).astype(jnp.bfloat16)

        for d in range(1, quads):
            target = lax.rem(quad + d, quads)
            copy = pltpu.make_async_remote_copy(
                stat.at[piece, slot_rows(target)], gathered.at[piece, slot_rows(me)],
                col_send.at[piece, d], col_recv.at[piece, d],
                device_id={"genome": target * QUAD + lane},
            )
            copy.start()
            col_copies[piece, d] = copy
        gathered[piece, slot_rows(me), :] = stat[piece, slot_rows(quad), :]
        forward(piece, 0)

    def pass_on(piece):
        for d in range(1, quads):
            col_copies[piece, d].wait_recv()
            forward(piece, d)

    out_copies = []

    def score(piece):
        for d in range(quads):
            for e in range(1, QUAD):
                quad_copies[piece, d, e].wait_recv()
        summed = jnp.dot(member[...], gathered[piece], preferred_element_type=jnp.float32)
        result[piece] = summed / count[...]
        copy = pltpu.make_async_copy(
            result.at[piece], out_ref.at[:, pl.ds(piece * PIECE, PIECE)], out_sem.at[piece]
        )
        copy.start()
        out_copies.append(copy)

    for piece in range(pieces):
        if piece == 0:
            span_copy = pltpu.make_async_remote_copy(
                own_span, pred_span, span_send, span_recv, device_id={"genome": right}
            )
            total = None
            for b in order:
                trim(b)
                fac_copies[b].wait()
                if b == 0:
                    span_copy.wait()
                    cover_both[:padded] = coverage(0, lower, upper)
                    cover_both[padded:] = coverage(0, *columns_of(pred_span[...]))
                else:
                    cover[b] = coverage(b, lower, upper)
                term = add_blocks([b], piece)
                total = term if total is None else total + term
                if b == order[0]:
                    pl.semaphore_wait(barrier, len(greeted))
                    span_copy.start()
            sums[piece] = total
            send_halo(piece)
        else:
            total = add_blocks([0], piece)
            send_halo(piece)
            finish_stat(piece - 1)
            if piece > 1:
                score(piece - 2)
            sums[piece] = total + add_blocks(order[:-1], piece)
            pass_on(piece - 1)
    finish_stat(pieces - 1)
    score(pieces - 2)
    pass_on(pieces - 1)
    score(pieces - 1)

    for piece in range(pieces):
        @pl.when(me > 0)
        def _():
            halo_copies[piece].wait_send()
    for copy in list(col_copies.values()) + list(quad_copies.values()):
        copy.wait_send()
    for copy in out_copies:
        copy.wait()


def local(factor, normals, block_len, block_rank, gene_span, gene_pathways):
    blocks, capacity, rank_cap = factor.shape
    sims = normals.shape[2]
    genes = gene_span.shape[0]
    total_genes, members = gene_pathways.shape
    n = lax.axis_size("genome")
    quads = n // QUAD
    rows = max(16, genes // quads)
    padded = quads * rows
    pieces = sims // PIECE
    path_rows = PATHWAYS // n
    hbm = pl.BlockSpec(memory_space=pltpu.HBM)
    dma = pltpu.SemaphoreType.DMA
    return pl.pallas_call(
        functools.partial(kernel, n, genes, rows),
        out_shape=jax.ShapeDtypeStruct((path_rows, sims), jnp.float32),
        in_specs=[hbm] * 6,
        out_specs=hbm,
        scratch_shapes=[
            pltpu.SMEM((blocks,), jnp.int32),
            pltpu.SMEM((blocks,), jnp.int32),
            pltpu.VMEM((2, genes), jnp.int32),
            pltpu.VMEM((members, total_genes), jnp.int32),
            pltpu.VMEM((blocks, capacity, rank_cap), jnp.bfloat16),
            pltpu.VMEM((blocks, rank_cap, sims), jnp.bfloat16),
            pltpu.VMEM((blocks, padded, capacity), jnp.bfloat16),
            pltpu.VMEM((2 * padded, capacity), jnp.bfloat16),
            pltpu.VMEM((pieces, padded, PIECE), jnp.float32),
            pltpu.VMEM((pieces, padded, PIECE), jnp.float32),
            pltpu.VMEM((pieces, padded, PIECE), jnp.float32),
            pltpu.VMEM((8, 128), jnp.float32),
            pltpu.VMEM((8, 128), jnp.float32),
            pltpu.VMEM((pieces, padded, PIECE), jnp.bfloat16),
            pltpu.VMEM((pieces, n * rows, PIECE), jnp.bfloat16),
            pltpu.VMEM((path_rows, n * rows), jnp.bfloat16),
            pltpu.VMEM((path_rows, 1), jnp.float32),
            pltpu.VMEM((pieces, path_rows, PIECE), jnp.float32),
            dma((4,)), dma((blocks,)), dma((blocks,)), dma, dma, dma((pieces,)), dma((pieces,)),
            dma((pieces, quads)), dma((pieces, quads)),
            dma((pieces, quads, QUAD)), dma((pieces, quads, QUAD)), dma((pieces,)),
        ],
        compiler_params=pltpu.CompilerParams(
            collective_id=0, has_side_effects=True, vmem_limit_bytes=56 * 1024 * 1024
        ),
        name="gene_sets",
    )(block_len, block_rank, gene_span.T, gene_pathways.T, factor, normals)


def solution(mesh):
    in_specs = (
        P(("groups", "genome"), None, None),
        P(("groups", "genome"), None, None),
        P(("groups", "genome")),
        P(("groups", "genome")),
        P(("groups", "genome"), None),
        P("groups", None),
    )
    out_specs = P(("groups", "genome"), None)
    return jax.shard_map(local, mesh=mesh, in_specs=in_specs, out_specs=out_specs, check_vma=False)
```

```python
import functools

import jax
import jax.numpy as jnp
from jax import lax
from jax.experimental import pallas as pl
from jax.experimental.pallas import tpu as pltpu
from jax.sharding import PartitionSpec as P

PATHWAYS = 4096
PIECE = 512
TILE = 512
QUAD = 4


def kernel(
    n, genes, rows,
    len_hbm, rank_hbm, span_hbm, paths_hbm, factor_ref, normals_ref,
    out_ref,
    len_ref, rank_ref, span_ref, paths_ref, fac, nrm, cover, cover_both,
    sums, partial, halo, own_span, pred_span, stat, gathered, member, count,
    small_sem, fac_sem, nrm_sem, span_send, span_recv, halo_send, halo_recv,
    col_send, col_recv, quad_send, quad_recv,
):
    quads = n // QUAD
    blocks, capacity, rank_cap = factor_ref.shape
    sims = normals_ref.shape[2]
    pieces = sims // PIECE
    local_vars = blocks * capacity
    padded = quads * rows
    path_rows, total_genes = out_ref.shape[0], paths_ref.shape[1]
    slots = n * rows
    me = lax.axis_index("genome")
    right, left = lax.rem(me + 1, n), lax.rem(me + n - 1, n)
    quad, lane = me // QUAD, lax.rem(me, QUAD)
    column = [lax.rem(quad + d, quads) * QUAD + lane for d in range(1, quads)]
    peers = [quad * QUAD + lax.rem(lane + e, QUAD) for e in range(1, QUAD)]

    barrier = pltpu.get_barrier_semaphore()
    greeted = [left, right] + column + peers
    for device in greeted:
        pl.semaphore_signal(barrier, inc=1, device_id={"genome": device})

    small = [
        pltpu.make_async_copy(source, target, small_sem.at[i])
        for i, (source, target) in enumerate(
            [(span_hbm, span_ref), (rank_hbm, rank_ref), (len_hbm, len_ref), (paths_hbm, paths_ref)]
        )
    ]
    for copy in small:
        copy.start()
    order = list(range(1, blocks)) + [0]
    fac_copies, nrm_copies = {}, {}
    for b in order:
        nrm_copies[b] = pltpu.make_async_copy(normals_ref.at[b], nrm.at[b], nrm_sem.at[b])
        fac_copies[b] = pltpu.make_async_copy(factor_ref.at[b], fac.at[b], fac_sem.at[b])
        nrm_copies[b].start()
        fac_copies[b].start()

    share = genes // quads
    row = lax.broadcasted_iota(jnp.int32, (padded, genes), 0)
    col = lax.broadcasted_iota(jnp.int32, (padded, genes), 1)
    within = lax.rem(row, rows)
    placed = (lax.div(row, rows) + quads * within == col) & (within < share)

    def columns_of(spans):
        lower = jnp.sum(jnp.where(placed, spans[0:1, :genes], 0.0), axis=1, keepdims=True)
        upper = jnp.sum(jnp.where(placed, spans[1:2, :genes], 0.0), axis=1, keepdims=True)
        return lower.astype(jnp.int32), upper.astype(jnp.int32)

    slot = lax.broadcasted_iota(jnp.int32, (1, slots), 1)
    first_gene = lax.div(slot, rows) * genes + lax.rem(slot, rows) * quads
    first_gene = jnp.where(lax.rem(slot, rows) < share, first_gene, total_genes)
    gene = lax.broadcasted_iota(jnp.int32, (total_genes, slots), 0)
    takes = (gene >= first_gene) & (gene < first_gene + quads)
    takes = takes.astype(jnp.float32).astype(jnp.bfloat16)
    own_span[...] = jnp.zeros_like(own_span)
    for copy in small:
        copy.wait()
    own_span[0:2, 0:genes] = span_ref[...].astype(jnp.float32)
    lower, upper = columns_of(own_span[...])
    named = paths_ref[pl.ds(lane, 1), :] - me * path_rows
    ids = lax.broadcasted_iota(jnp.int32, (path_rows, total_genes), 0)
    names = (named == ids).astype(jnp.float32).astype(jnp.bfloat16)
    chosen = jnp.dot(names, takes, preferred_element_type=jnp.float32)
    count[...] = jnp.sum(chosen, axis=1, keepdims=True)
    member[...] = chosen.astype(jnp.bfloat16)

    def trim(b):
        nrm_copies[b].wait()
        kept = lax.broadcasted_iota(jnp.int32, (rank_cap, sims), 0) < rank_ref[b]
        nrm[b] = jnp.where(kept, nrm[b].astype(jnp.float32), 0.0).astype(jnp.bfloat16)

    def coverage(b, low, high):
        start = me * local_vars + b * capacity
        place = start + lax.broadcasted_iota(jnp.int32, (padded, capacity), 1)
        inside = (place >= low) & (place < jnp.minimum(high, start + len_ref[b]))
        return inside.astype(jnp.float32).astype(jnp.bfloat16)

    def coloured(b, piece, first):
        return jnp.dot(
            fac[b, pl.ds(first, TILE), :],
            nrm[b, :, pl.ds(piece * PIECE, PIECE)],
            preferred_element_type=jnp.float32,
        )

    def add_blocks(chain, piece):
        steps = [(b, first) for b in chain for first in range(0, capacity, TILE)]
        totals = {}
        for b, first in steps:
            values = coloured(b, piece, first)
            squares = (values * values).astype(jnp.bfloat16)
            rows_of = cover_both if b == 0 else cover.at[b]
            term = jnp.dot(
                rows_of[:, pl.ds(first, TILE)], squares, preferred_element_type=jnp.float32
            )
            totals[b] = totals[b] + term if b in totals else term
        kept = None
        for b, total in totals.items():
            if b == 0:
                partial[piece] = total[padded:]
                total = total[:padded]
            kept = total if kept is None else kept + total
        return kept

    halo_copies = [
        pltpu.make_async_remote_copy(
            partial.at[piece], halo.at[piece], halo_send.at[piece], halo_recv.at[piece],
            device_id={"genome": left},
        )
        for piece in range(pieces)
    ]

    def send_halo(piece):
        @pl.when(me > 0)
        def _():
            halo_copies[piece].start()

    scale = 1.0 / capacity
    col_copies, quad_copies = {}, {}

    def slot_rows(index):
        return pl.ds(pl.multiple_of(index * rows, rows), rows)

    def forward(piece, d):
        source = lax.rem(quad + quads - d, quads) * QUAD + lane
        block = gathered.at[piece, slot_rows(source)]
        for e in range(1, QUAD):
            copy = pltpu.make_async_remote_copy(
                block, block, quad_send.at[piece, d, e], quad_recv.at[piece, d, e],
                device_id={"genome": peers[e - 1]},
            )
            copy.start()
            quad_copies[piece, d, e] = copy

    def finish_stat(piece):
        @pl.when(me < n - 1)
        def _():
            halo_copies[piece].wait_recv()
            stat[piece] = ((sums[piece] + halo[piece]) * scale).astype(jnp.bfloat16)

        @pl.when(me == n - 1)
        def _():
            stat[piece] = (sums[piece] * scale).astype(jnp.bfloat16)

        for d in range(1, quads):
            target = lax.rem(quad + d, quads)
            copy = pltpu.make_async_remote_copy(
                stat.at[piece, slot_rows(target)], gathered.at[piece, slot_rows(me)],
                col_send.at[piece, d], col_recv.at[piece, d],
                device_id={"genome": target * QUAD + lane},
            )
            copy.start()
            col_copies[piece, d] = copy
        gathered[piece, slot_rows(me), :] = stat[piece, slot_rows(quad), :]
        forward(piece, 0)

    def pass_on(piece):
        for d in range(1, quads):
            col_copies[piece, d].wait_recv()
            forward(piece, d)

    def score(piece):
        for d in range(quads):
            for e in range(1, QUAD):
                quad_copies[piece, d, e].wait_recv()
        summed = jnp.dot(member[...], gathered[piece], preferred_element_type=jnp.float32)
        out_ref[:, pl.ds(piece * PIECE, PIECE)] = summed / count[...]

    for piece in range(pieces):
        if piece == 0:
            span_copy = pltpu.make_async_remote_copy(
                own_span, pred_span, span_send, span_recv, device_id={"genome": right}
            )
            total = None
            for b in order:
                trim(b)
                fac_copies[b].wait()
                if b == 0:
                    span_copy.wait()
                    cover_both[:padded] = coverage(0, lower, upper)
                    cover_both[padded:] = coverage(0, *columns_of(pred_span[...]))
                else:
                    cover[b] = coverage(b, lower, upper)
                term = add_blocks([b], piece)
                total = term if total is None else total + term
                if b == order[0]:
                    pl.semaphore_wait(barrier, len(greeted))
                    span_copy.start()
            sums[piece] = total
            send_halo(piece)
        else:
            total = add_blocks([0], piece)
            send_halo(piece)
            finish_stat(piece - 1)
            if piece > 1:
                score(piece - 2)
            sums[piece] = total + add_blocks(order[:-1], piece)
            pass_on(piece - 1)
    finish_stat(pieces - 1)
    score(pieces - 2)
    pass_on(pieces - 1)
    score(pieces - 1)

    for piece in range(pieces):
        @pl.when(me > 0)
        def _():
            halo_copies[piece].wait_send()
    for copy in list(col_copies.values()) + list(quad_copies.values()):
        copy.wait_send()


def local(factor, normals, block_len, block_rank, gene_span, gene_pathways):
    blocks, capacity, rank_cap = factor.shape
    sims = normals.shape[2]
    genes = gene_span.shape[0]
    total_genes, members = gene_pathways.shape
    n = lax.axis_size("genome")
    quads = n // QUAD
    rows = max(16, genes // quads)
    padded = quads * rows
    pieces = sims // PIECE
    path_rows = PATHWAYS // n
    hbm = pl.BlockSpec(memory_space=pltpu.HBM)
    dma = pltpu.SemaphoreType.DMA
    return pl.pallas_call(
        functools.partial(kernel, n, genes, rows),
        out_shape=jax.ShapeDtypeStruct((path_rows, sims), jnp.float32),
        in_specs=[hbm] * 6,
        out_specs=pl.BlockSpec(memory_space=pltpu.VMEM),
        scratch_shapes=[
            pltpu.SMEM((blocks,), jnp.int32),
            pltpu.SMEM((blocks,), jnp.int32),
            pltpu.VMEM((2, genes), jnp.int32),
            pltpu.VMEM((members, total_genes), jnp.int32),
            pltpu.VMEM((blocks, capacity, rank_cap), jnp.bfloat16),
            pltpu.VMEM((blocks, rank_cap, sims), jnp.bfloat16),
            pltpu.VMEM((blocks, padded, capacity), jnp.bfloat16),
            pltpu.VMEM((2 * padded, capacity), jnp.bfloat16),
            pltpu.VMEM((pieces, padded, PIECE), jnp.float32),
            pltpu.VMEM((pieces, padded, PIECE), jnp.float32),
            pltpu.VMEM((pieces, padded, PIECE), jnp.float32),
            pltpu.VMEM((8, 128), jnp.float32),
            pltpu.VMEM((8, 128), jnp.float32),
            pltpu.VMEM((pieces, padded, PIECE), jnp.bfloat16),
            pltpu.VMEM((pieces, n * rows, PIECE), jnp.bfloat16),
            pltpu.VMEM((path_rows, n * rows), jnp.bfloat16),
            pltpu.VMEM((path_rows, 1), jnp.float32),
            dma((4,)), dma((blocks,)), dma((blocks,)), dma, dma, dma((pieces,)), dma((pieces,)),
            dma((pieces, quads)), dma((pieces, quads)),
            dma((pieces, quads, QUAD)), dma((pieces, quads, QUAD)),
        ],
        compiler_params=pltpu.CompilerParams(
            collective_id=0, has_side_effects=True, vmem_limit_bytes=50 * 1024 * 1024
        ),
        name="gene_sets",
    )(block_len, block_rank, gene_span.T, gene_pathways.T, factor, normals)


def solution(mesh):
    in_specs = (
        P(("groups", "genome"), None, None),
        P(("groups", "genome"), None, None),
        P(("groups", "genome")),
        P(("groups", "genome")),
        P(("groups", "genome"), None),
        P("groups", None),
    )
    out_specs = P(("groups", "genome"), None)
    return jax.shard_map(local, mesh=mesh, in_specs=in_specs, out_specs=out_specs, check_vma=False)
```

```python
import functools

import jax
import jax.numpy as jnp
from jax import lax
from jax.experimental import pallas as pl
from jax.experimental.pallas import tpu as pltpu
from jax.sharding import PartitionSpec as P

PATHWAYS = 4096
PIECE = 512
TILE = 2048
QUAD = 4


def kernel(
    n, genes, rows,
    len_hbm, rank_hbm, span_hbm, paths_hbm, factor_ref, normals_ref,
    out_ref, count_hbm,
    len_ref, rank_ref, span_ref, paths_ref, fac, nrm, cover, cover_both,
    sums, partial, halo, own_span, pred_span, stat, gathered, member, count, result,
    small_sem, fac_sem, nrm_sem, span_send, span_recv, halo_send, halo_recv,
    col_send, col_recv, quad_send, quad_recv, out_sem,
):
    quads = n // QUAD
    blocks, capacity, rank_cap = factor_ref.shape
    sims = normals_ref.shape[2]
    pieces = sims // PIECE
    local_vars = blocks * capacity
    padded = quads * rows
    path_rows, total_genes = out_ref.shape[0], paths_ref.shape[1]
    slots = n * rows
    me = lax.axis_index("genome")
    right, left = lax.rem(me + 1, n), lax.rem(me + n - 1, n)
    quad, lane = me // QUAD, lax.rem(me, QUAD)
    column = [lax.rem(quad + d, quads) * QUAD + lane for d in range(1, quads)]
    peers = [quad * QUAD + lax.rem(lane + e, QUAD) for e in range(1, QUAD)]

    barrier = pltpu.get_barrier_semaphore()
    greeted = [left, right] + column + peers
    for device in greeted:
        pl.semaphore_signal(barrier, inc=1, device_id={"genome": device})

    small = [
        pltpu.make_async_copy(source, target, small_sem.at[i])
        for i, (source, target) in enumerate(
            [(span_hbm, span_ref), (rank_hbm, rank_ref), (len_hbm, len_ref), (paths_hbm, paths_ref)]
        )
    ]
    for copy in small:
        copy.start()
    order = list(range(1, blocks)) + [0]
    fac_copies, nrm_copies = {}, {}
    for b in order:
        nrm_copies[b] = pltpu.make_async_copy(normals_ref.at[b], nrm.at[b], nrm_sem.at[b])
        fac_copies[b] = pltpu.make_async_copy(factor_ref.at[b], fac.at[b], fac_sem.at[b])
        nrm_copies[b].start()
        fac_copies[b].start()

    share = genes // quads
    row = lax.broadcasted_iota(jnp.int32, (padded, genes), 0)
    col = lax.broadcasted_iota(jnp.int32, (padded, genes), 1)
    within = lax.rem(row, rows)
    placed = (lax.div(row, rows) + quads * within == col) & (within < share)

    def columns_of(spans):
        lower = jnp.sum(jnp.where(placed, spans[0:1, :genes], 0.0), axis=1, keepdims=True)
        upper = jnp.sum(jnp.where(placed, spans[1:2, :genes], 0.0), axis=1, keepdims=True)
        return lower.astype(jnp.int32), upper.astype(jnp.int32)

    slot = lax.broadcasted_iota(jnp.int32, (1, slots), 1)
    first_gene = lax.div(slot, rows) * genes + lax.rem(slot, rows) * quads
    first_gene = jnp.where(lax.rem(slot, rows) < share, first_gene, total_genes)
    gene = lax.broadcasted_iota(jnp.int32, (total_genes, slots), 0)
    takes = (gene >= first_gene) & (gene < first_gene + quads)
    takes = takes.astype(jnp.float32).astype(jnp.bfloat16)
    own_span[...] = jnp.zeros_like(own_span)
    for copy in small:
        copy.wait()
    own_span[0:2, 0:genes] = span_ref[...].astype(jnp.float32)
    lower, upper = columns_of(own_span[...])
    named = paths_ref[pl.ds(lane, 1), :] - me * path_rows
    ids = lax.broadcasted_iota(jnp.int32, (path_rows, total_genes), 0)
    names = (named == ids).astype(jnp.float32).astype(jnp.bfloat16)
    chosen = jnp.dot(names, takes, preferred_element_type=jnp.float32)
    count[...] = jnp.broadcast_to(jnp.sum(chosen, axis=1, keepdims=True), count.shape)
    member[...] = chosen.astype(jnp.bfloat16)

    count_copy = pltpu.make_async_copy(count, count_hbm, out_sem.at[pieces])
    count_copy.start()

    def trim(b):
        nrm_copies[b].wait()
        kept = lax.broadcasted_iota(jnp.int32, (rank_cap, sims), 0) < rank_ref[b]
        nrm[b] = jnp.where(kept, nrm[b].astype(jnp.float32), 0.0).astype(jnp.bfloat16)

    def coverage(b, low, high):
        start = me * local_vars + b * capacity
        place = start + lax.broadcasted_iota(jnp.int32, (padded, capacity), 1)
        inside = (place >= low) & (place < jnp.minimum(high, start + len_ref[b]))
        return inside.astype(jnp.float32).astype(jnp.bfloat16)

    def coloured(b, piece, first):
        return jnp.dot(
            fac[b, pl.ds(first, TILE), :],
            nrm[b, :, pl.ds(piece * PIECE, PIECE)],
            preferred_element_type=jnp.float32,
        )

    def add_blocks(chain, piece):
        steps = [(b, first) for b in chain for first in range(0, capacity, TILE)]
        totals = {}
        for b, first in steps:
            values = coloured(b, piece, first)
            squares = (values * values).astype(jnp.bfloat16)
            rows_of = cover_both if b == 0 else cover.at[b]
            term = jnp.dot(
                rows_of[:, pl.ds(first, TILE)], squares, preferred_element_type=jnp.float32
            )
            totals[b] = totals[b] + term if b in totals else term
        kept = None
        for b, total in totals.items():
            if b == 0:
                partial[piece] = total[padded:]
                total = total[:padded]
            kept = total if kept is None else kept + total
        return kept

    halo_copies = [
        pltpu.make_async_remote_copy(
            partial.at[piece], halo.at[piece], halo_send.at[piece], halo_recv.at[piece],
            device_id={"genome": left},
        )
        for piece in range(pieces)
    ]

    def send_halo(piece):
        @pl.when(me > 0)
        def _():
            halo_copies[piece].start()

    scale = 1.0 / capacity
    col_copies, quad_copies = {}, {}

    def slot_rows(index):
        return pl.ds(pl.multiple_of(index * rows, rows), rows)

    def forward(piece, d):
        source = lax.rem(quad + quads - d, quads) * QUAD + lane
        block = gathered.at[piece, slot_rows(source)]
        for e in range(1, QUAD):
            copy = pltpu.make_async_remote_copy(
                block, block, quad_send.at[piece, d, e], quad_recv.at[piece, d, e],
                device_id={"genome": peers[e - 1]},
            )
            copy.start()
            quad_copies[piece, d, e] = copy

    def finish_stat(piece):
        @pl.when(me < n - 1)
        def _():
            halo_copies[piece].wait_recv()
            stat[piece] = ((sums[piece] + halo[piece]) * scale).astype(jnp.bfloat16)

        @pl.when(me == n - 1)
        def _():
            stat[piece] = (sums[piece] * scale).astype(jnp.bfloat16)

        for d in range(1, quads):
            target = lax.rem(quad + d, quads)
            copy = pltpu.make_async_remote_copy(
                stat.at[piece, slot_rows(target)], gathered.at[piece, slot_rows(me)],
                col_send.at[piece, d], col_recv.at[piece, d],
                device_id={"genome": target * QUAD + lane},
            )
            copy.start()
            col_copies[piece, d] = copy
        gathered[piece, slot_rows(me), :] = stat[piece, slot_rows(quad), :]
        forward(piece, 0)

    def pass_on(piece):
        for d in range(1, quads):
            col_copies[piece, d].wait_recv()
            forward(piece, d)

    out_copies = [count_copy]

    def score(piece):
        for d in range(quads):
            for e in range(1, QUAD):
                quad_copies[piece, d, e].wait_recv()
        result[piece] = jnp.dot(
            member[...], gathered[piece], preferred_element_type=jnp.float32
        )
        copy = pltpu.make_async_copy(
            result.at[piece], out_ref.at[:, pl.ds(piece * PIECE, PIECE)], out_sem.at[piece]
        )
        copy.start()
        out_copies.append(copy)

    for piece in range(pieces):
        if piece == 0:
            span_copy = pltpu.make_async_remote_copy(
                own_span, pred_span, span_send, span_recv, device_id={"genome": right}
            )
            total = None
            for b in order:
                trim(b)
                fac_copies[b].wait()
                if b == 0:
                    span_copy.wait()
                    cover_both[:padded] = coverage(0, lower, upper)
                    cover_both[padded:] = coverage(0, *columns_of(pred_span[...]))
                else:
                    cover[b] = coverage(b, lower, upper)
                term = add_blocks([b], piece)
                total = term if total is None else total + term
                if b == order[0]:
                    pl.semaphore_wait(barrier, len(greeted))
                    span_copy.start()
            sums[piece] = total
            send_halo(piece)
        else:
            total = add_blocks([0], piece)
            send_halo(piece)
            finish_stat(piece - 1)
            if piece > 1:
                score(piece - 2)
            sums[piece] = total + add_blocks(order[:-1], piece)
            pass_on(piece - 1)
    finish_stat(pieces - 1)
    score(pieces - 2)
    pass_on(pieces - 1)
    score(pieces - 1)

    for piece in range(pieces):
        @pl.when(me > 0)
        def _():
            halo_copies[piece].wait_send()
    for copy in list(col_copies.values()) + list(quad_copies.values()):
        copy.wait_send()
    for copy in out_copies:
        copy.wait()


def local(factor, normals, block_len, block_rank, gene_span, gene_pathways):
    blocks, capacity, rank_cap = factor.shape
    sims = normals.shape[2]
    genes = gene_span.shape[0]
    total_genes, members = gene_pathways.shape
    n = lax.axis_size("genome")
    quads = n // QUAD
    rows = max(16, genes // quads)
    padded = quads * rows
    pieces = sims // PIECE
    path_rows = PATHWAYS // n
    hbm = pl.BlockSpec(memory_space=pltpu.HBM)
    dma = pltpu.SemaphoreType.DMA
    summed, count = pl.pallas_call(
        functools.partial(kernel, n, genes, rows),
        out_shape=[
            jax.ShapeDtypeStruct((path_rows, sims), jnp.float32),
            jax.ShapeDtypeStruct((path_rows, 128), jnp.float32),
        ],
        in_specs=[hbm] * 6,
        out_specs=[hbm, hbm],
        scratch_shapes=[
            pltpu.SMEM((blocks,), jnp.int32),
            pltpu.SMEM((blocks,), jnp.int32),
            pltpu.VMEM((2, genes), jnp.int32),
            pltpu.VMEM((members, total_genes), jnp.int32),
            pltpu.VMEM((blocks, capacity, rank_cap), jnp.bfloat16),
            pltpu.VMEM((blocks, rank_cap, sims), jnp.bfloat16),
            pltpu.VMEM((blocks, padded, capacity), jnp.bfloat16),
            pltpu.VMEM((2 * padded, capacity), jnp.bfloat16),
            pltpu.VMEM((pieces, padded, PIECE), jnp.float32),
            pltpu.VMEM((pieces, padded, PIECE), jnp.float32),
            pltpu.VMEM((pieces, padded, PIECE), jnp.float32),
            pltpu.VMEM((8, 128), jnp.float32),
            pltpu.VMEM((8, 128), jnp.float32),
            pltpu.VMEM((pieces, padded, PIECE), jnp.bfloat16),
            pltpu.VMEM((pieces, n * rows, PIECE), jnp.bfloat16),
            pltpu.VMEM((path_rows, n * rows), jnp.bfloat16),
            pltpu.VMEM((path_rows, 128), jnp.float32),
            pltpu.VMEM((pieces, path_rows, PIECE), jnp.float32),
            dma((4,)), dma((blocks,)), dma((blocks,)), dma, dma, dma((pieces,)), dma((pieces,)),
            dma((pieces, quads)), dma((pieces, quads)),
            dma((pieces, quads, QUAD)), dma((pieces, quads, QUAD)), dma((pieces + 1,)),
        ],
        compiler_params=pltpu.CompilerParams(
            collective_id=0, has_side_effects=True, vmem_limit_bytes=60 * 1024 * 1024
        ),
        name="gene_sets",
    )(block_len, block_rank, gene_span.T, gene_pathways.T, factor, normals)
    return summed / jnp.concatenate([count] * (sims // 128), axis=1)


def solution(mesh):
    in_specs = (
        P(("groups", "genome"), None, None),
        P(("groups", "genome"), None, None),
        P(("groups", "genome")),
        P(("groups", "genome")),
        P(("groups", "genome"), None),
        P("groups", None),
    )
    out_specs = P(("groups", "genome"), None)
    return jax.shard_map(local, mesh=mesh, in_specs=in_specs, out_specs=out_specs, check_vma=False)
```

```python
import functools

import jax
import jax.numpy as jnp
from jax import lax
from jax.experimental import pallas as pl
from jax.experimental.pallas import tpu as pltpu
from jax.sharding import PartitionSpec as P

PATHWAYS = 4096
PIECE = 512
TILE = 2048
QUAD = 4


def kernel(
    n, genes, rows,
    len_hbm, rank_hbm, span_hbm, paths_hbm, factor_ref, normals_ref,
    out_ref,
    len_ref, rank_ref, span_ref, paths_ref, fac, nrm, cover, cover_both,
    sums, partial, halo, own_span, pred_span, stat, gathered, member, count,
    small_sem, fac_sem, nrm_sem, span_send, span_recv, halo_send, halo_recv,
    col_send, col_recv, quad_send, quad_recv,
):
    quads = n // QUAD
    blocks, capacity, rank_cap = factor_ref.shape
    sims = normals_ref.shape[2]
    pieces = sims // PIECE
    local_vars = blocks * capacity
    padded = quads * rows
    path_rows, total_genes = out_ref.shape[0], paths_ref.shape[1]
    slots = n * rows
    me = lax.axis_index("genome")
    right, left = lax.rem(me + 1, n), lax.rem(me + n - 1, n)
    quad, lane = me // QUAD, lax.rem(me, QUAD)
    column = [lax.rem(quad + d, quads) * QUAD + lane for d in range(1, quads)]
    peers = [quad * QUAD + lax.rem(lane + e, QUAD) for e in range(1, QUAD)]

    barrier = pltpu.get_barrier_semaphore()
    greeted = [left, right] + column + peers
    for device in greeted:
        pl.semaphore_signal(barrier, inc=1, device_id={"genome": device})

    small = [
        pltpu.make_async_copy(source, target, small_sem.at[i])
        for i, (source, target) in enumerate(
            [(span_hbm, span_ref), (rank_hbm, rank_ref), (len_hbm, len_ref), (paths_hbm, paths_ref)]
        )
    ]
    for copy in small:
        copy.start()
    order = list(range(1, blocks)) + [0]
    fac_copies, nrm_copies = {}, {}
    for b in order:
        nrm_copies[b] = pltpu.make_async_copy(normals_ref.at[b], nrm.at[b], nrm_sem.at[b])
        fac_copies[b] = pltpu.make_async_copy(factor_ref.at[b], fac.at[b], fac_sem.at[b])
        nrm_copies[b].start()
        fac_copies[b].start()

    share = genes // quads
    row = lax.broadcasted_iota(jnp.int32, (padded, genes), 0)
    col = lax.broadcasted_iota(jnp.int32, (padded, genes), 1)
    within = lax.rem(row, rows)
    placed = (lax.div(row, rows) + quads * within == col) & (within < share)

    def columns_of(spans):
        lower = jnp.sum(jnp.where(placed, spans[0:1, :genes], 0.0), axis=1, keepdims=True)
        upper = jnp.sum(jnp.where(placed, spans[1:2, :genes], 0.0), axis=1, keepdims=True)
        return lower.astype(jnp.int32), upper.astype(jnp.int32)

    slot = lax.broadcasted_iota(jnp.int32, (1, slots), 1)
    first_gene = lax.div(slot, rows) * genes + lax.rem(slot, rows) * quads
    first_gene = jnp.where(lax.rem(slot, rows) < share, first_gene, total_genes)
    gene = lax.broadcasted_iota(jnp.int32, (total_genes, slots), 0)
    takes = (gene >= first_gene) & (gene < first_gene + quads)
    takes = takes.astype(jnp.float32).astype(jnp.bfloat16)
    own_span[...] = jnp.zeros_like(own_span)
    for copy in small:
        copy.wait()
    own_span[0:2, 0:genes] = span_ref[...].astype(jnp.float32)
    lower, upper = columns_of(own_span[...])
    named = paths_ref[pl.ds(lane, 1), :] - me * path_rows
    ids = lax.broadcasted_iota(jnp.int32, (path_rows, total_genes), 0)
    names = (named == ids).astype(jnp.float32).astype(jnp.bfloat16)
    chosen = jnp.dot(names, takes, preferred_element_type=jnp.float32)
    count[...] = jnp.sum(chosen, axis=1, keepdims=True)
    member[...] = chosen.astype(jnp.bfloat16)

    def trim(b):
        nrm_copies[b].wait()
        kept = lax.broadcasted_iota(jnp.int32, (rank_cap, sims), 0) < rank_ref[b]
        nrm[b] = jnp.where(kept, nrm[b].astype(jnp.float32), 0.0).astype(jnp.bfloat16)

    def coverage(b, low, high):
        start = me * local_vars + b * capacity
        place = start + lax.broadcasted_iota(jnp.int32, (padded, capacity), 1)
        inside = (place >= low) & (place < jnp.minimum(high, start + len_ref[b]))
        return inside.astype(jnp.float32).astype(jnp.bfloat16)

    def coloured(b, piece, first):
        return jnp.dot(
            fac[b, pl.ds(first, TILE), :],
            nrm[b, :, pl.ds(piece * PIECE, PIECE)],
            preferred_element_type=jnp.float32,
        )

    def add_blocks(chain, piece):
        steps = [(b, first) for b in chain for first in range(0, capacity, TILE)]
        totals = {}
        for b, first in steps:
            values = coloured(b, piece, first)
            squares = (values * values).astype(jnp.bfloat16)
            rows_of = cover_both if b == 0 else cover.at[b]
            term = jnp.dot(
                rows_of[:, pl.ds(first, TILE)], squares, preferred_element_type=jnp.float32
            )
            totals[b] = totals[b] + term if b in totals else term
        kept = None
        for b, total in totals.items():
            if b == 0:
                partial[piece] = total[padded:]
                total = total[:padded]
            kept = total if kept is None else kept + total
        return kept

    halo_copies = [
        pltpu.make_async_remote_copy(
            partial.at[piece], halo.at[piece], halo_send.at[piece], halo_recv.at[piece],
            device_id={"genome": left},
        )
        for piece in range(pieces)
    ]

    def send_halo(piece):
        @pl.when(me > 0)
        def _():
            halo_copies[piece].start()

    scale = 1.0 / capacity
    col_copies, quad_copies = {}, {}

    def slot_rows(index):
        return pl.ds(pl.multiple_of(index * rows, rows), rows)

    def forward(piece, d):
        source = lax.rem(quad + quads - d, quads) * QUAD + lane
        block = gathered.at[piece, slot_rows(source)]
        for e in range(1, QUAD):
            copy = pltpu.make_async_remote_copy(
                block, block, quad_send.at[piece, d, e], quad_recv.at[piece, d, e],
                device_id={"genome": peers[e - 1]},
            )
            copy.start()
            quad_copies[piece, d, e] = copy

    def finish_stat(piece):
        @pl.when(me < n - 1)
        def _():
            halo_copies[piece].wait_recv()
            stat[piece] = ((sums[piece] + halo[piece]) * scale).astype(jnp.bfloat16)

        @pl.when(me == n - 1)
        def _():
            stat[piece] = (sums[piece] * scale).astype(jnp.bfloat16)

        for d in range(1, quads):
            target = lax.rem(quad + d, quads)
            copy = pltpu.make_async_remote_copy(
                stat.at[piece, slot_rows(target)], gathered.at[piece, slot_rows(me)],
                col_send.at[piece, d], col_recv.at[piece, d],
                device_id={"genome": target * QUAD + lane},
            )
            copy.start()
            col_copies[piece, d] = copy
        gathered[piece, slot_rows(me), :] = stat[piece, slot_rows(quad), :]
        forward(piece, 0)

    def pass_on(piece):
        for d in range(1, quads):
            col_copies[piece, d].wait_recv()
            forward(piece, d)

    def score(piece):
        for d in range(quads):
            for e in range(1, QUAD):
                quad_copies[piece, d, e].wait_recv()
        summed = jnp.dot(member[...], gathered[piece], preferred_element_type=jnp.float32)
        out_ref[:, pl.ds(piece * PIECE, PIECE)] = summed / count[...]

    for piece in range(pieces):
        if piece == 0:
            span_copy = pltpu.make_async_remote_copy(
                own_span, pred_span, span_send, span_recv, device_id={"genome": right}
            )
            total = None
            for b in order:
                trim(b)
                fac_copies[b].wait()
                if b == 0:
                    span_copy.wait()
                    cover_both[:padded] = coverage(0, lower, upper)
                    cover_both[padded:] = coverage(0, *columns_of(pred_span[...]))
                else:
                    cover[b] = coverage(b, lower, upper)
                term = add_blocks([b], piece)
                total = term if total is None else total + term
                if b == order[0]:
                    pl.semaphore_wait(barrier, len(greeted))
                    span_copy.start()
            sums[piece] = total
            send_halo(piece)
        else:
            total = add_blocks([0], piece)
            send_halo(piece)
            finish_stat(piece - 1)
            if piece > 1:
                score(piece - 2)
            for b in order[:-1]:
                total += add_blocks([b], piece)
                if b == order[0]:
                    pass_on(piece - 1)
            sums[piece] = total
    finish_stat(pieces - 1)
    pass_on(pieces - 1)
    score(pieces - 2)
    score(pieces - 1)

    for piece in range(pieces):
        @pl.when(me > 0)
        def _():
            halo_copies[piece].wait_send()
    for copy in list(col_copies.values()) + list(quad_copies.values()):
        copy.wait_send()


def local(factor, normals, block_len, block_rank, gene_span, gene_pathways):
    blocks, capacity, rank_cap = factor.shape
    sims = normals.shape[2]
    genes = gene_span.shape[0]
    total_genes, members = gene_pathways.shape
    n = lax.axis_size("genome")
    quads = n // QUAD
    rows = max(16, genes // quads)
    padded = quads * rows
    pieces = sims // PIECE
    path_rows = PATHWAYS // n
    hbm = pl.BlockSpec(memory_space=pltpu.HBM)
    dma = pltpu.SemaphoreType.DMA
    return pl.pallas_call(
        functools.partial(kernel, n, genes, rows),
        out_shape=jax.ShapeDtypeStruct((path_rows, sims), jnp.float32),
        in_specs=[hbm] * 6,
        out_specs=pl.BlockSpec(memory_space=pltpu.VMEM),
        scratch_shapes=[
            pltpu.SMEM((blocks,), jnp.int32),
            pltpu.SMEM((blocks,), jnp.int32),
            pltpu.VMEM((2, genes), jnp.int32),
            pltpu.VMEM((members, total_genes), jnp.int32),
            pltpu.VMEM((blocks, capacity, rank_cap), jnp.bfloat16),
            pltpu.VMEM((blocks, rank_cap, sims), jnp.bfloat16),
            pltpu.VMEM((blocks, padded, capacity), jnp.bfloat16),
            pltpu.VMEM((2 * padded, capacity), jnp.bfloat16),
            pltpu.VMEM((pieces, padded, PIECE), jnp.float32),
            pltpu.VMEM((pieces, padded, PIECE), jnp.float32),
            pltpu.VMEM((pieces, padded, PIECE), jnp.float32),
            pltpu.VMEM((8, 128), jnp.float32),
            pltpu.VMEM((8, 128), jnp.float32),
            pltpu.VMEM((pieces, padded, PIECE), jnp.bfloat16),
            pltpu.VMEM((pieces, n * rows, PIECE), jnp.bfloat16),
            pltpu.VMEM((path_rows, n * rows), jnp.bfloat16),
            pltpu.VMEM((path_rows, 1), jnp.float32),
            dma((4,)), dma((blocks,)), dma((blocks,)), dma, dma, dma((pieces,)), dma((pieces,)),
            dma((pieces, quads)), dma((pieces, quads)),
            dma((pieces, quads, QUAD)), dma((pieces, quads, QUAD)),
        ],
        compiler_params=pltpu.CompilerParams(
            collective_id=0, has_side_effects=True, vmem_limit_bytes=60 * 1024 * 1024
        ),
        name="gene_sets",
    )(block_len, block_rank, gene_span.T, gene_pathways.T, factor, normals)


def solution(mesh):
    in_specs = (
        P(("groups", "genome"), None, None),
        P(("groups", "genome"), None, None),
        P(("groups", "genome")),
        P(("groups", "genome")),
        P(("groups", "genome"), None),
        P("groups", None),
    )
    out_specs = P(("groups", "genome"), None)
    return jax.shard_map(local, mesh=mesh, in_specs=in_specs, out_specs=out_specs, check_vma=False)
```
